32 devices in a mesh: rows: 8 (over z, y), irrep: 4 (over x, core).
Axes of the slice: x: 2, y: 2, z: 4, core: 2. Of those that a mesh axis runs over, the one named last changes fastest.
Arguments:
- coefficients: float32 [4, 2560, 2560], P('irrep', 'rows'), may hold values from -6 to 6
- block_codes: int32 [4, 4, 4, 320], P('irrep'), may hold values from -1 to 19, as said below
- tile_bank: float32 [4, 4, 8, 128, 128], P('irrep'), may hold values from -0.125 to 0.125
Outputs:
- sigma_vector: float32 [4, 2560, 2560], P('irrep', 'rows')
The draws below stay inside these ranges and needn't reach their ends.
Inputs may be any that keep to these rules, and one draw needn't show every extreme that they name: Fields 0 and 1 of block_codes[g, k] are block numbers below 20 for k = 0, 3 and below 20 for k = 1, 2; the first of them list the diagonal blocks 0, 1, ... in order, so every block row holds a listed block; field 2 is a tile number below 8; field 3 is -1 or +1.
All inputs are finite; a program needn't handle non-finite values.
Results may differ from the reference program's by a relative error of at most 0.0001.
Values sent between devices are 32-bit elements; how exact they have to be, the bound alone decides.
A program may use at most 256 MiB of HBM per device.

```python
import jax
import jax.numpy as jnp
from jax import lax

NA = 2560
NB = 2560
BLK = 128
NNZ = 320
NT = 8
NIRR = 4


def draw_block_codes(key, part):
    base_key = jax.random.fold_in(key, 11)
    position = jnp.arange(NNZ, dtype=jnp.int32)[None, :]
    operators = []
    for which_op in range(4):
        op_key = jax.random.fold_in(base_key, which_op)
        keys_here = jax.random.split(op_key, 4)
        if which_op == 0 or which_op == 3:
            block_count = NB // BLK
        else:
            block_count = NA // BLK
        row_draw = jax.random.randint(keys_here[0], (NIRR, NNZ), 0, block_count, dtype=jnp.int32)
        col_draw = jax.random.randint(keys_here[1], (NIRR, NNZ), 0, block_count, dtype=jnp.int32)
        row_block = jnp.where(position < block_count, position, row_draw)
        col_block = jnp.where(position < block_count, position, col_draw)
        tile_index = jax.random.randint(keys_here[2], (NIRR, NNZ), 0, NT, dtype=jnp.int32)
        sign_draw = jax.random.randint(keys_here[3], (NIRR, NNZ), 0, 2, dtype=jnp.int32) * 2 - 1
        sign_value = jnp.where(position == 0, jnp.int32(-1), sign_draw)
        operators.append(jnp.stack([row_block, col_block, tile_index, sign_value], axis=1))
    return jnp.stack(operators, axis=1).astype(jnp.int32)


def levels(own_key, extent, cuts, smallest, high):
    gain = 1.0
    for axis_at, shards_of in cuts:
        steps = jax.random.uniform(jax.random.fold_in(jax.random.fold_in(own_key, 6), axis_at), (shards_of,), jnp.float32, smallest / len(cuts), high / len(cuts))
        gain = gain * jnp.repeat(jnp.exp(steps), extent[axis_at] // shards_of).reshape((-1,) + (1,) * (len(extent) - 1 - axis_at))
    return gain


def bell_draw(rng, extent, spread, bound, shards=(), kind=jnp.bfloat16):
    values = jax.random.normal(rng, extent, jnp.float32) * spread
    if len(shards) > 0:
        values = levels(rng, extent, shards, -0.22, 0.18) * values
    return jnp.clip(values, min=-bound, max=bound).astype(kind)


def setup_inputs(seed: int = 0) -> dict:
    streams_of = jax.random.split(jax.random.key(seed), 4)
    coefficients = bell_draw(streams_of[0], (NIRR, NA, NB), 1.0, 6.0, ((0, 4), (1, 8)), jnp.float32)
    block_codes = draw_block_codes(jax.random.fold_in(streams_of[3], 71), 0)
    tile_bank = bell_draw(streams_of[2], (NIRR, 4, NT, BLK, BLK), (NNZ * BLK * BLK // NB) ** -0.5, 0.125, ((0, 4),), jnp.float32)
    return dict(coefficients=coefficients, block_codes=block_codes, tile_bank=tile_bank)


highest = lax.Precision.HIGHEST


def apply_operator(values, block_codes, tile_bank):
    tile_size = tile_bank.shape[-1]
    tile_count = tile_bank.shape[0]
    block_count = values.shape[-1] // tile_size
    pieces = values.reshape(values.shape[0], block_count, tile_size)
    every_tile = jnp.einsum("rbq,tpq->rbtp", pieces, tile_bank, precision=highest)
    every_tile = every_tile.reshape(values.shape[0], block_count * tile_count, tile_size)
    flat_index = (block_codes[1] * tile_count + block_codes[2]).astype(jnp.int32)
    product = jnp.take(every_tile, flat_index, axis=1)
    placed = jnp.where(block_codes[0][:, None] == jnp.arange(block_count, dtype=jnp.int32)[None, :], block_codes[3][:, None].astype(jnp.float32), jnp.float32(0.0))
    result = jnp.einsum("rkp,kb->rbp", product, placed, precision=highest)
    return result.reshape(values.shape[0], block_count * tile_size)


def reference(coefficients, block_codes, tile_bank):
    outputs = []
    for irrep_index in range(NIRR):
        partner_index = (irrep_index + NIRR // 2) % NIRR
        own_block = coefficients[irrep_index]
        codes_here = block_codes[irrep_index]
        tiles_here = tile_bank[irrep_index]
        beta_term = apply_operator(own_block, codes_here[0], tiles_here[0])
        alpha_term = apply_operator(own_block.T, codes_here[1], tiles_here[1]).T
        mixed = apply_operator(coefficients[partner_index], codes_here[3], tiles_here[3])
        cross_term = apply_operator(mixed.T, codes_here[2], tiles_here[2]).T
        outputs.append(beta_term + alpha_term + cross_term)
    return jnp.stack(outputs)
```

```python
import jax
import jax.numpy as jnp
from jax import lax
from jax.experimental import pallas as pl
from jax.experimental.pallas import tpu as pltpu
from jax.sharding import PartitionSpec as P

CONTRACT_LAST = (((1,), (1,)), ((), ()))


def from_partner(shard, axis, bit):
    return lax.ppermute(shard, axis, [(i, i ^ 1 << bit) for i in range(lax.axis_size(axis))])


def operator_kernel(codes, values, tiles, result, matrix, halves):
    rows, extent = values.shape
    tile_size = tiles.shape[-1]
    step = 2 * tile_size if extent % (2 * tile_size) == 0 else tile_size

    high = values[...].astype(jnp.bfloat16)
    halves[:rows, :] = high
    halves[rows:, :] = (values[...] - high.astype(jnp.float32)).astype(jnp.bfloat16)

    def clear(i, _):
        matrix[pl.ds(pl.multiple_of(i * tile_size, tile_size), tile_size), :] = jnp.zeros(
            (tile_size, extent), jnp.float32
        )
        return 0

    lax.fori_loop(0, extent // tile_size, clear, 0)

    def place(m, _):
        where = (
            pl.ds(pl.multiple_of(codes[0, m] * tile_size, tile_size), tile_size),
            pl.ds(pl.multiple_of(codes[1, m] * tile_size, tile_size), tile_size),
        )
        matrix[where] += codes[3, m].astype(jnp.float32) * tiles[codes[2, m]]
        return 0

    lax.fori_loop(0, codes.shape[1], place, 0)

    def multiply(i, _):
        part = pl.ds(pl.multiple_of(i * step, step), step)
        block = matrix[part, :]
        block_high = block.astype(jnp.bfloat16)
        block_low = (block - block_high.astype(jnp.float32)).astype(jnp.bfloat16)
        both = lax.dot_general(
            halves[...], block_high, CONTRACT_LAST, preferred_element_type=jnp.float32
        )
        rest = lax.dot_general(
            halves[:rows, :], block_low, CONTRACT_LAST, preferred_element_type=jnp.float32
        )
        result[:, part] = both[:rows] + (both[rows:] + rest)
        return 0

    lax.fori_loop(0, extent // step, multiply, 0)


def apply_operator(values, block_codes, tile_bank):
    rows, extent = values.shape
    vmem = pl.BlockSpec(memory_space=pltpu.VMEM)
    return pl.pallas_call(
        operator_kernel,
        out_shape=jax.ShapeDtypeStruct((rows, extent), jnp.float32),
        in_specs=[pl.BlockSpec(memory_space=pltpu.SMEM), vmem, vmem],
        out_specs=vmem,
        scratch_shapes=[
            pltpu.VMEM((extent, extent), jnp.float32),
            pltpu.VMEM((2 * rows, extent), jnp.bfloat16),
        ],
        compiler_params=pltpu.CompilerParams(vmem_limit_bytes=56 * 2**20),
        cost_estimate=pl.CostEstimate(
            flops=6 * rows * extent * extent, bytes_accessed=8 * rows * extent, transcendentals=0
        ),
    )(block_codes, values, tile_bank)


def applied(values, block_codes, tile_bank, which_op):
    return jnp.stack(
        [
            apply_operator(values[g], block_codes[g, which_op], tile_bank[g, which_op])
            for g in range(values.shape[0])
        ]
    )


def body(coefficients, block_codes, tile_bank):
    flipped_bit = lax.axis_size("irrep").bit_length() - 2
    partner = from_partner(coefficients, "irrep", flipped_bit)
    by_beta = jnp.swapaxes(coefficients, 1, 2)
    beta_term = applied(coefficients, block_codes, tile_bank, 0)
    columns = lax.all_to_all(by_beta, "rows", split_axis=1, concat_axis=2, tiled=True)
    mixed = applied(partner, block_codes, tile_bank, 3)
    cross_columns = lax.all_to_all(
        jnp.swapaxes(mixed, 1, 2), "rows", split_axis=1, concat_axis=2, tiled=True
    )
    alpha_columns = applied(columns, block_codes, tile_bank, 1) + applied(
        cross_columns, block_codes, tile_bank, 2
    )
    returned = lax.all_to_all(alpha_columns, "rows", split_axis=2, concat_axis=1, tiled=True)
    return beta_term + jnp.swapaxes(returned, 1, 2)


def solution(mesh):
    in_specs = (
        P("irrep", "rows", None),
        P("irrep", None, None, None),
        P("irrep", None, None, None, None),
    )
    out_specs = P("irrep", "rows", None)
    return jax.shard_map(body, mesh=mesh, in_specs=in_specs, out_specs=out_specs, check_vma=False)
```

```python
import jax
import jax.numpy as jnp
from jax import lax
from jax.experimental import pallas as pl
from jax.experimental.pallas import tpu as pltpu
from jax.sharding import PartitionSpec as P

CONTRACT_LAST = (((1,), (1,)), ((), ()))


def from_partner(shard, axis, bit):
    return lax.ppermute(shard, axis, [(i, i ^ 1 << bit) for i in range(lax.axis_size(axis))])


def operator_kernel(codes, values, tiles, *refs):
    *base, result, matrix, halves = refs
    rows, extent = values.shape
    tile_size = tiles.shape[-1]
    step = 2 * tile_size if extent % (2 * tile_size) == 0 else tile_size

    high = values[...].astype(jnp.bfloat16)
    halves[:rows, :] = high
    halves[rows:, :] = (values[...] - high.astype(jnp.float32)).astype(jnp.bfloat16)

    def clear(i, _):
        matrix[pl.ds(pl.multiple_of(i * tile_size, tile_size), tile_size), :] = jnp.zeros(
            (tile_size, extent), jnp.float32
        )
        return 0

    lax.fori_loop(0, extent // tile_size, clear, 0)

    def place(m, _):
        where = (
            pl.ds(pl.multiple_of(codes[0, m] * tile_size, tile_size), tile_size),
            pl.ds(pl.multiple_of(codes[1, m] * tile_size, tile_size), tile_size),
        )
        matrix[where] += codes[3, m].astype(jnp.float32) * tiles[codes[2, m]]
        return 0

    lax.fori_loop(0, codes.shape[1], place, 0)

    def multiply(i, _):
        part = pl.ds(pl.multiple_of(i * step, step), step)
        block = matrix[part, :]
        block_high = block.astype(jnp.bfloat16)
        block_low = (block - block_high.astype(jnp.float32)).astype(jnp.bfloat16)
        both = lax.dot_general(
            halves[...], block_high, CONTRACT_LAST, preferred_element_type=jnp.float32
        )
        rest = lax.dot_general(
            halves[:rows, :], block_low, CONTRACT_LAST, preferred_element_type=jnp.float32
        )
        product = both[:rows] + (both[rows:] + rest)
        result[:, part] = base[0][:, part] + product if base else product
        return 0

    lax.fori_loop(0, extent // step, multiply, 0)


def apply_operator(values, block_codes, tile_bank, *base):
    rows, extent = values.shape
    vmem = pl.BlockSpec(memory_space=pltpu.VMEM)
    return pl.pallas_call(
        operator_kernel,
        out_shape=jax.ShapeDtypeStruct((rows, extent), jnp.float32),
        in_specs=[pl.BlockSpec(memory_space=pltpu.SMEM)] + [vmem] * (2 + len(base)),
        out_specs=vmem,
        scratch_shapes=[
            pltpu.VMEM((extent, extent), jnp.float32),
            pltpu.VMEM((2 * rows, extent), jnp.bfloat16),
        ],
        compiler_params=pltpu.CompilerParams(vmem_limit_bytes=56 * 2**20),
        cost_estimate=pl.CostEstimate(
            flops=6 * rows * extent * extent, bytes_accessed=8 * rows * extent, transcendentals=0
        ),
    )(block_codes, values, tile_bank, *base)


def column_plan(extent, count, rows, tile_size):
    parts = extent // (count * tile_size)
    rest = extent // count - parts * tile_size
    if parts and rest == 0:
        return parts, tile_size, 0
    narrow = rest // max(parts, 1)
    if parts and rest % parts == 0 and tile_size % narrow == 0 and rows % (8 * tile_size // narrow) == 0:
        return parts, tile_size, narrow
    return 1, 0, extent // count


def fold(blocks, width):
    count, rows, narrow = blocks.shape
    times = width // narrow
    folded = blocks.reshape(count, times, rows // times, narrow)
    return jnp.swapaxes(folded, 1, 2).reshape(count, rows // times, width)


def unfold(packed, narrow):
    count, rows, width = packed.shape
    folded = packed.reshape(count, rows, width // narrow, narrow)
    return jnp.swapaxes(folded, 1, 2).reshape(count, rows * (width // narrow), narrow)


def exchange(packed):
    return lax.all_to_all(packed, "rows", split_axis=0, concat_axis=0, tiled=True)


def one_irrep(own, codes, bank, partner_codes, partner_tiles, bit):
    count = lax.axis_size("rows")
    rows, extent = own.shape
    parts, wide, narrow = column_plan(extent, count, rows, bank.shape[-1])
    width = wide + narrow

    def join(whole, rest):
        pieces = [whole] if wide else []
        if narrow:
            pieces.append(fold(rest, wide or narrow))
        return jnp.concatenate(pieces, axis=1)

    def split(packed):
        rest = unfold(packed[:, rows if wide else 0 :], narrow) if narrow else None
        return packed[:, :rows] if wide else None, rest

    def outgoing(values, part):
        def blocks(start, size):
            start += part * count * size
            return jnp.swapaxes(values[:, start : start + count * size].reshape(rows, count, size), 0, 1)

        return join(blocks(0, wide), blocks(parts * count * wide, narrow))

    def by_beta(arrived):
        blocks = [x for x in split(arrived) if x is not None]
        return jnp.concatenate([x.reshape(count * rows, x.shape[-1]).T for x in blocks], axis=0)

    def by_alpha(columns):
        return join(
            columns[:wide].T.reshape(count, rows, wide), columns[wide:].T.reshape(count, rows, narrow)
        )

    def home(blocks):
        return jnp.swapaxes(blocks, 0, 1).reshape(rows, count * blocks.shape[-1])

    packed, own = lax.optimization_barrier(
        (jnp.concatenate([outgoing(own, p) for p in range(parts)], axis=1), own)
    )
    sent = exchange(packed)
    length = sent.shape[1] // parts
    mixed = apply_operator(own, partner_codes, partner_tiles)
    crossing = [from_partner(outgoing(mixed, p), "irrep", bit) for p in range(parts)]
    sent, crossing[0] = lax.optimization_barrier((sent, crossing[0]))
    columns = jnp.concatenate(
        [by_beta(sent[:, p * length : (p + 1) * length]) for p in range(parts)], axis=0
    )
    beta_term = apply_operator(own, codes[0], bank[0])
    alpha_own = apply_operator(columns, codes[1], bank[1])
    crossed = [exchange(x) for x in crossing]
    returned = []
    for p in range(parts):
        total = by_alpha(
            apply_operator(by_beta(crossed[p]), codes[2], bank[2], alpha_own[p * width : (p + 1) * width])
        )
        if p + 1 < parts:
            crossed[p + 1], total = lax.optimization_barrier((crossed[p + 1], total))
        returned.append(split(exchange(total)))
    pieces = [home(x[k]) for k in range(2) for x in returned if x[k] is not None]
    return beta_term + jnp.concatenate(pieces, axis=1)


def body(coefficients, block_codes, tile_bank):
    bit = lax.axis_size("irrep").bit_length() - 2
    partner_tiles = from_partner(tile_bank[:, 3], "irrep", bit)
    partner_codes = from_partner(block_codes[:, 3], "irrep", bit)
    return jnp.stack(
        [
            one_irrep(
                coefficients[g], block_codes[g], tile_bank[g], partner_codes[g], partner_tiles[g], bit
            )
            for g in range(coefficients.shape[0])
        ]
    )


def solution(mesh):
    in_specs = (
        P("irrep", "rows", None),
        P("irrep", None, None, None),
        P("irrep", None, None, None, None),
    )
    out_specs = P("irrep", "rows", None)
    return jax.shard_map(body, mesh=mesh, in_specs=in_specs, out_specs=out_specs, check_vma=False)
```

```python
import jax
import jax.numpy as jnp
from jax import lax
from jax.experimental import pallas as pl
from jax.experimental.pallas import tpu as pltpu
from jax.sharding import PartitionSpec as P

CONTRACT_LAST = (((1,), (1,)), ((), ()))


def from_partner(shard, axis, bit):
    return lax.ppermute(shard, axis, [(i, i ^ 1 << bit) for i in range(lax.axis_size(axis))])


def operator_kernel(codes, values, tiles, *refs):
    *base, result, matrix, halves = refs
    rows, extent = values.shape
    tile_size = tiles.shape[-1]
    step = 2 * tile_size if extent % (2 * tile_size) == 0 else tile_size

    high = values[...].astype(jnp.bfloat16)
    halves[:rows, :] = high
    halves[rows:, :] = (values[...] - high.astype(jnp.float32)).astype(jnp.bfloat16)

    def clear(i, _):
        matrix[pl.ds(pl.multiple_of(i * tile_size, tile_size), tile_size), :] = jnp.zeros(
            (tile_size, extent), jnp.float32
        )
        return 0

    lax.fori_loop(0, extent // tile_size, clear, 0)

    def place(m, _):
        where = (
            pl.ds(pl.multiple_of(codes[0, m] * tile_size, tile_size), tile_size),
            pl.ds(pl.multiple_of(codes[1, m] * tile_size, tile_size), tile_size),
        )
        matrix[where] += codes[3, m].astype(jnp.float32) * tiles[codes[2, m]]
        return 0

    lax.fori_loop(0, codes.shape[1], place, 0)

    def multiply(i, _):
        part = pl.ds(pl.multiple_of(i * step, step), step)
        block = matrix[part, :]
        block_high = block.astype(jnp.bfloat16)
        block_low = (block - block_high.astype(jnp.float32)).astype(jnp.bfloat16)
        both = lax.dot_general(
            halves[...], block_high, CONTRACT_LAST, preferred_element_type=jnp.float32
        )
        rest = lax.dot_general(
            halves[:rows, :], block_low, CONTRACT_LAST, preferred_element_type=jnp.float32
        )
        product = both[:rows] + (both[rows:] + rest)
        result[:, part] = base[0][:, part] + product if base else product
        return 0

    lax.fori_loop(0, extent // step, multiply, 0)


def apply_operator(values, block_codes, tile_bank, *base):
    rows, extent = values.shape
    vmem = pl.BlockSpec(memory_space=pltpu.VMEM)
    return pl.pallas_call(
        operator_kernel,
        out_shape=jax.ShapeDtypeStruct((rows, extent), jnp.float32),
        in_specs=[pl.BlockSpec(memory_space=pltpu.SMEM)] + [vmem] * (2 + len(base)),
        out_specs=vmem,
        scratch_shapes=[
            pltpu.VMEM((extent, extent), jnp.float32),
            pltpu.VMEM((2 * rows, extent), jnp.bfloat16),
        ],
        compiler_params=pltpu.CompilerParams(vmem_limit_bytes=56 * 2**20),
        cost_estimate=pl.CostEstimate(
            flops=6 * rows * extent * extent, bytes_accessed=8 * rows * extent, transcendentals=0
        ),
    )(block_codes, values, tile_bank, *base)


def column_plan(extent, count, rows, tile_size):
    parts = extent // (count * tile_size)
    rest = extent // count - parts * tile_size
    if parts and rest == 0:
        return parts, tile_size, 0
    narrow = rest // max(parts, 1)
    if parts and rest % parts == 0 and tile_size % narrow == 0 and rows % (8 * tile_size // narrow) == 0:
        return parts, tile_size, narrow
    return 1, 0, extent // count


def fold(blocks, width):
    count, rows, narrow = blocks.shape
    times = width // narrow
    folded = blocks.reshape(count, times, rows // times, narrow)
    return jnp.swapaxes(folded, 1, 2).reshape(count, rows // times, width)


def unfold(packed, narrow):
    count, rows, width = packed.shape
    folded = packed.reshape(count, rows, width // narrow, narrow)
    return jnp.swapaxes(folded, 1, 2).reshape(count, rows * (width // narrow), narrow)


def exchange(packed):
    return lax.all_to_all(packed, "rows", split_axis=0, concat_axis=0, tiled=True)


def one_irrep(own, codes, bank, partner_codes, partner_tiles, bit):
    count = lax.axis_size("rows")
    rows, extent = own.shape
    parts, wide, narrow = column_plan(extent, count, rows, bank.shape[-1])
    width = wide + narrow

    def join(whole, rest):
        pieces = [whole] if wide else []
        if narrow:
            pieces.append(fold(rest, wide or narrow))
        return jnp.concatenate(pieces, axis=1)

    def split(packed):
        rest = unfold(packed[:, rows if wide else 0 :], narrow) if narrow else None
        return packed[:, :rows] if wide else None, rest

    def outgoing(values, part):
        def blocks(start, size):
            start += part * count * size
            return jnp.swapaxes(values[:, start : start + count * size].reshape(rows, count, size), 0, 1)

        return join(blocks(0, wide), blocks(parts * count * wide, narrow))

    def by_beta(arrived):
        blocks = [x for x in split(arrived) if x is not None]
        return jnp.concatenate([x.reshape(count * rows, x.shape[-1]).T for x in blocks], axis=0)

    def by_alpha(columns):
        return join(
            columns[:wide].T.reshape(count, rows, wide), columns[wide:].T.reshape(count, rows, narrow)
        )

    def home(blocks):
        return jnp.swapaxes(blocks, 0, 1).reshape(rows, count * blocks.shape[-1])

    packed, own = lax.optimization_barrier(
        (jnp.concatenate([outgoing(own, p) for p in range(parts)], axis=1), own)
    )
    sent = exchange(packed)
    length = sent.shape[1] // parts
    mixed = apply_operator(own, partner_codes, partner_tiles)
    leaving = [outgoing(mixed, p) for p in range(parts)]
    crossing = [from_partner(x, "irrep", bit) for x in leaving]
    columns = jnp.concatenate(
        [by_beta(sent[:, p * length : (p + 1) * length]) for p in range(parts)], axis=0
    )
    crossing[0] = lax.optimization_barrier((crossing[0], columns, leaving))[0]
    beta_term = apply_operator(own, codes[0], bank[0])
    alpha_own = apply_operator(columns, codes[1], bank[1])
    crossed = [exchange(x) for x in crossing]
    returned = []
    for p in range(parts):
        total = by_alpha(
            apply_operator(by_beta(crossed[p]), codes[2], bank[2], alpha_own[p * width : (p + 1) * width])
        )
        if p + 1 < parts:
            crossed[p + 1], total = lax.optimization_barrier((crossed[p + 1], total))
        returned.append(split(exchange(total)))
    pieces = [home(x[k]) for k in range(2) for x in returned if x[k] is not None]
    return beta_term + jnp.concatenate(pieces, axis=1)


def body(coefficients, block_codes, tile_bank):
    bit = lax.axis_size("irrep").bit_length() - 2
    partner_tiles = from_partner(tile_bank[:, 3], "irrep", bit)
    partner_codes = from_partner(block_codes[:, 3], "irrep", bit)
    return jnp.stack(
        [
            one_irrep(
                coefficients[g], block_codes[g], tile_bank[g], partner_codes[g], partner_tiles[g], bit
            )
            for g in range(coefficients.shape[0])
        ]
    )


def solution(mesh):
    in_specs = (
        P("irrep", "rows", None),
        P("irrep", None, None, None),
        P("irrep", None, None, None, None),
    )
    out_specs = P("irrep", "rows", None)
    return jax.shard_map(body, mesh=mesh, in_specs=in_specs, out_specs=out_specs, check_vma=False)
```

```python
import jax
import jax.numpy as jnp
from jax import lax
from jax.experimental import pallas as pl
from jax.experimental.pallas import tpu as pltpu
from jax.sharding import PartitionSpec as P

CONTRACT_LAST = (((1,), (1,)), ((), ()))


def from_partner(shard, axis, bit):
    return lax.ppermute(shard, axis, [(i, i ^ 1 << bit) for i in range(lax.axis_size(axis))])


def operator_kernel(codes, values, tiles, *refs):
    *base, result, matrix, halves = refs
    rows, extent = values.shape
    tile_size = tiles.shape[-1]
    step = 2 * tile_size if extent % (2 * tile_size) == 0 else tile_size

    high = values[...].astype(jnp.bfloat16)
    halves[:rows, :] = high
    halves[rows:, :] = (values[...] - high.astype(jnp.float32)).astype(jnp.bfloat16)

    def clear(i, _):
        matrix[pl.ds(pl.multiple_of(i * tile_size, tile_size), tile_size), :] = jnp.zeros(
            (tile_size, extent), jnp.float32
        )
        return 0

    lax.fori_loop(0, extent // tile_size, clear, 0)

    def place(m, _):
        where = (
            pl.ds(pl.multiple_of(codes[0, m] * tile_size, tile_size), tile_size),
            pl.ds(pl.multiple_of(codes[1, m] * tile_size, tile_size), tile_size),
        )
        matrix[where] += codes[3, m].astype(jnp.float32) * tiles[codes[2, m]]
        return 0

    lax.fori_loop(0, codes.shape[1], place, 0)

    def multiply(i, _):
        part = pl.ds(pl.multiple_of(i * step, step), step)
        block = matrix[part, :]
        block_high = block.astype(jnp.bfloat16)
        block_low = (block - block_high.astype(jnp.float32)).astype(jnp.bfloat16)
        both = lax.dot_general(
            halves[...], block_high, CONTRACT_LAST, preferred_element_type=jnp.float32
        )
        rest = lax.dot_general(
            halves[:rows, :], block_low, CONTRACT_LAST, preferred_element_type=jnp.float32
        )
        product = both[:rows] + (both[rows:] + rest)
        result[:, part] = base[0][:, part] + product if base else product
        return 0

    lax.fori_loop(0, extent // step, multiply, 0)


def apply_operator(values, block_codes, tile_bank, *base):
    rows, extent = values.shape
    vmem = pl.BlockSpec(memory_space=pltpu.VMEM)
    return pl.pallas_call(
        operator_kernel,
        out_shape=jax.ShapeDtypeStruct((rows, extent), jnp.float32),
        in_specs=[pl.BlockSpec(memory_space=pltpu.SMEM)] + [vmem] * (2 + len(base)),
        out_specs=vmem,
        scratch_shapes=[
            pltpu.VMEM((extent, extent), jnp.float32),
            pltpu.VMEM((2 * rows, extent), jnp.bfloat16),
        ],
        compiler_params=pltpu.CompilerParams(vmem_limit_bytes=56 * 2**20),
        cost_estimate=pl.CostEstimate(
            flops=6 * rows * extent * extent, bytes_accessed=8 * rows * extent, transcendentals=0
        ),
    )(block_codes, values, tile_bank, *base)


def column_plan(extent, count, rows, tile_size):
    parts = extent // (count * tile_size)
    rest = extent // count - parts * tile_size
    if parts and rest == 0:
        return parts, tile_size, 0
    narrow = rest // max(parts, 1)
    if parts and rest % parts == 0 and tile_size % narrow == 0 and rows % (8 * tile_size // narrow) == 0:
        return parts, tile_size, narrow
    return 1, 0, extent // count


def fold(blocks, width):
    count, rows, narrow = blocks.shape
    times = width // narrow
    folded = blocks.reshape(count, times, rows // times, narrow)
    return jnp.swapaxes(folded, 1, 2).reshape(count, rows // times, width)


def unfold(packed, narrow):
    count, rows, width = packed.shape
    folded = packed.reshape(count, rows, width // narrow, narrow)
    return jnp.swapaxes(folded, 1, 2).reshape(count, rows * (width // narrow), narrow)


def exchange(packed):
    return lax.all_to_all(packed, "rows", split_axis=0, concat_axis=0, tiled=True)


def one_irrep(own, codes, bank, partner_codes, partner_tiles, bit):
    count = lax.axis_size("rows")
    rows, extent = own.shape
    parts, wide, narrow = column_plan(extent, count, rows, bank.shape[-1])
    width = wide + narrow

    def join(whole, rest):
        pieces = [whole] if wide else []
        if narrow:
            pieces.append(fold(rest, wide or narrow))
        return jnp.concatenate(pieces, axis=1)

    def split(packed):
        rest = unfold(packed[:, rows if wide else 0 :], narrow) if narrow else None
        return packed[:, :rows] if wide else None, rest

    def outgoing(values, part):
        def blocks(start, size):
            start += part * count * size
            return jnp.swapaxes(values[:, start : start + count * size].reshape(rows, count, size), 0, 1)

        return join(blocks(0, wide), blocks(parts * count * wide, narrow))

    def by_beta(arrived):
        blocks = [x for x in split(arrived) if x is not None]
        return jnp.concatenate([x.reshape(count * rows, x.shape[-1]).T for x in blocks], axis=0)

    def by_alpha(columns):
        return join(
            columns[:wide].T.reshape(count, rows, wide), columns[wide:].T.reshape(count, rows, narrow)
        )

    def home(blocks):
        return jnp.swapaxes(blocks, 0, 1).reshape(rows, count * blocks.shape[-1])

    packed, own = lax.optimization_barrier(
        (jnp.concatenate([outgoing(own, p) for p in range(parts)], axis=1), own)
    )
    sent = exchange(packed)
    length = sent.shape[1] // parts
    mixed = apply_operator(own, partner_codes, partner_tiles)
    leaving = [outgoing(mixed, p) for p in range(parts)]
    crossing = [from_partner(x, "irrep", bit) for x in leaving]
    columns = jnp.concatenate(
        [by_beta(sent[:, p * length : (p + 1) * length]) for p in range(parts)], axis=0
    )
    crossing[0] = lax.optimization_barrier((crossing[0], columns, leaving))[0]
    beta_term = apply_operator(own, codes[0], bank[0])
    alpha_own = apply_operator(columns, codes[1], bank[1])
    crossed = [exchange(x) for x in crossing]
    returned = []
    for p in range(parts):
        total = by_alpha(
            apply_operator(by_beta(crossed[p]), codes[2], bank[2], alpha_own[p * width : (p + 1) * width])
        )
        if p + 1 < parts:
            crossed[p + 1], total = lax.optimization_barrier((crossed[p + 1], total))
        returned.append(split(exchange(total)))
    pieces = [home(x[k]) for k in range(2) for x in returned if x[k] is not None]
    return beta_term + jnp.concatenate(pieces, axis=1)


def body(coefficients, block_codes, tile_bank):
    bit = lax.axis_size("irrep").bit_length() - 2
    tiles, codes, coefficients = lax.optimization_barrier(
        (tile_bank[:, 3], block_codes[:, 3], coefficients)
    )
    partner_tiles = from_partner(tiles, "irrep", bit)
    partner_codes = from_partner(codes, "irrep", bit)
    return jnp.stack(
        [
            one_irrep(
                coefficients[g], block_codes[g], tile_bank[g], partner_codes[g], partner_tiles[g], bit
            )
            for g in range(coefficients.shape[0])
        ]
    )


def solution(mesh):
    in_specs = (
        P("irrep", "rows", None),
        P("irrep", None, None, None),
        P("irrep", None, None, None, None),
    )
    out_specs = P("irrep", "rows", None)
    return jax.shard_map(body, mesh=mesh, in_specs=in_specs, out_specs=out_specs, check_vma=False)
```
